32 devices in a mesh: lat: 8 (over z, y), lon: 4 (over x, core).
Axes of the slice: x: 2, y: 2, z: 4, core: 2. Of those that a mesh axis runs over, the one named last changes fastest.
Arguments:
- thickness: float32 [2, 704, 5760], P(None, 'lat', 'lon'), may hold values from 0.5 to 1.5
- zonal_wind: float32 [2, 704, 5760], P(None, 'lat', 'lon'), may hold values from -3 to 3
- merid_wind: float32 [2, 704, 5760], P(None, 'lat', 'lon'), may hold values from -3 to 3
- tracers: float32 [8, 2, 704, 5760], P(None, None, 'lat', 'lon'), may hold values from 0.1 to 2
- cutoffs: int32 [176], replicated, may hold values from 64 to 512
Outputs:
- new_thickness: float32 [2, 704, 5760], P(None, 'lat', 'lon')
- new_zonal: float32 [2, 704, 5760], P(None, 'lat', 'lon')
- new_merid: float32 [2, 704, 5760], P(None, 'lat', 'lon')
- tracer_mass: float32 [8, 2, 704, 5760], P(None, None, 'lat', 'lon')
The draws below stay inside these ranges and needn't reach their ends.
All inputs are finite; a program needn't handle non-finite values.
Results may differ from the reference program's by a relative error of at most 0.0003.
Values sent between devices are 32-bit elements; how exact they have to be, the bound alone decides.
A program may use at most 192 MiB of HBM per device.

```python
import math
import jax
import jax.numpy as jnp
from jax import lax

NLON = 5760
NTR = 8
LEV = 2
KMAX = 512
SUBSTEPS = 3
NLAT = 704
POLAR = 88
KLO = 64


def draw_cutoffs(key, part):
    key = jax.random.fold_in(key, 7)
    total_slots = 2 * POLAR
    slot_index = jnp.arange(total_slots, dtype=jnp.int32)
    from_pole = jnp.where(slot_index < POLAR, slot_index, total_slots - 1 - slot_index)
    base_cut = KLO + (KMAX - KLO) * from_pole // POLAR
    jitter_span = max(KMAX // 16, 1)
    jitter = jax.random.randint(key, (total_slots,), -jitter_span, jitter_span + 1, dtype=jnp.int32)
    cut_values = jnp.clip(base_cut + jitter, KLO, KMAX)
    cut_values = cut_values.at[0].set(KLO).at[POLAR - 1].set(KMAX)
    return cut_values.astype(jnp.int32)


def levels(rng, dims, cuts, low, top_value):
    def one(axis_at, blocks):
        draws = jax.random.uniform(jax.random.fold_in(jax.random.fold_in(rng, 6), axis_at), (blocks,), jnp.float32, low / len(cuts), top_value / len(cuts))
        return jnp.repeat(jnp.exp(draws), dims[axis_at] // blocks).reshape((-1,) + (1,) * (len(dims) - axis_at - 1))

    level = one(*cuts[0])
    for cut in cuts[1:]:
        level = level * one(*cut)
    return level


def bell_draw(stream_key, shape, width, reach, shards=(), kind=jnp.bfloat16):
    loudness = levels(stream_key, shape, shards, -0.22, 0.18) if shards else 1.0
    drawn = jax.random.normal(stream_key, shape, jnp.float32) * width * loudness
    return jnp.minimum(jnp.maximum(drawn, -reach), reach).astype(kind)


def setup_inputs(seed: int = 0) -> dict:
    arg_keys = jax.random.split(jax.random.key(seed), 6)
    thickness = jnp.clip(0.5 + 1.0 * jax.random.uniform(arg_keys[0], (LEV, NLAT, NLON), jnp.float32) ** levels(arg_keys[0], (LEV, NLAT, NLON), ((1, 8), (2, 4)), -0.2, 0.2), 0.5, 1.5)
    zonal_wind = bell_draw(arg_keys[1], (LEV, NLAT, NLON), 0.5, 3.0, ((1, 8), (2, 4)), jnp.float32)
    merid_wind = bell_draw(arg_keys[2], (LEV, NLAT, NLON), 0.5, 3.0, ((1, 8), (2, 4)), jnp.float32)
    tracers = jnp.clip(jnp.exp(math.log(2.0) - 2.9957323 * jax.random.uniform(arg_keys[3], (NTR, LEV, NLAT, NLON), jnp.float32) ** levels(arg_keys[3], (NTR, LEV, NLAT, NLON), ((2, 8), (3, 4)), -0.2, 0.2)), 0.1, 2.0)
    cutoffs = draw_cutoffs(jax.random.fold_in(arg_keys[5], 71), 0)
    return {"thickness": thickness, "zonal_wind": zonal_wind, "merid_wind": merid_wind, "tracers": tracers, "cutoffs": cutoffs}


LAT_EDGE = 85.0 * math.pi / 180.0
PRESSURE_PUSH = 0.08
DIVERGE_RATE = 0.08
COURANT_RATE = 0.3


def center_cos(global_rows, total_rows):
    return jnp.cos(((2 * global_rows + 1).astype(jnp.float32) / total_rows - 1.0) * LAT_EDGE)


def face_cos(global_rows, total_rows):
    return jnp.cos(((2 * global_rows + 2).astype(jnp.float32) / total_rows - 1.0) * LAT_EDGE)


def fourier_basis(columns, length, modes):
    waves = jnp.arange(modes, dtype=jnp.int32)
    phase = (columns[:, None] * waves[None, :]) % length
    angle = phase.astype(jnp.float32) * (2.0 * math.pi / length)
    return jnp.concatenate([jnp.cos(angle), jnp.sin(angle)], axis=1)


def spectral_weights(row_cut, length, modes):
    waves = jnp.arange(modes, dtype=jnp.int32)
    scaled = jnp.where(waves == 0, 1.0, 2.0).astype(jnp.float32) / length
    keep_mode = waves[None, :] < row_cut[:, None]
    weights = jnp.where(keep_mode, scaled[None, :], jnp.zeros_like(scaled)[None, :])
    return jnp.concatenate([weights, weights], axis=1)


def ppm_faces(values, courant, along_dim, length):
    def part(offset):
        return lax.slice_in_dim(values, 2 + offset, 3 + offset + length, axis=along_dim)
    back_two, back_one, center, ahead_one, ahead_two, ahead_three = [part(offset) for offset in range(-2, 4)]
    left_edge = (7.0 / 12.0) * (back_one + center) - (1.0 / 12.0) * (back_two + ahead_one)
    middle_edge = (7.0 / 12.0) * (center + ahead_one) - (1.0 / 12.0) * (back_one + ahead_two)
    right_edge = (7.0 / 12.0) * (ahead_one + ahead_two) - (1.0 / 12.0) * (center + ahead_three)
    slope_here = middle_edge - left_edge
    curve_here = 6.0 * center - 3.0 * (left_edge + middle_edge)
    slope_next = right_edge - middle_edge
    curve_next = 6.0 * ahead_one - 3.0 * (middle_edge + right_edge)
    clipped = jnp.clip(courant, -1.0, 1.0)
    upwind = middle_edge - 0.5 * clipped * (slope_here - (1.0 - clipped * (2.0 / 3.0)) * curve_here)
    downwind = middle_edge - 0.5 * clipped * (slope_next + (1.0 + clipped * (2.0 / 3.0)) * curve_next)
    return jnp.where(clipped > 0.0, upwind, downwind)


def wrap_pad(values, margin):
    beside_all = jnp.concatenate([values[..., -margin:], values, values[..., :margin]], axis=-1)
    spread = [(0, 0)] * (values.ndim - 2) + [(margin, margin), (0, 0)]
    return jnp.pad(beside_all, spread)


def polar_filter(stacked, cutoffs):
    south = stacked[:, :, :POLAR, :]
    north = stacked[:, :, NLAT - POLAR:, :]
    caps = jnp.concatenate([south, north], axis=2)
    shape = caps.shape
    flat = caps.reshape(-1, NLON)
    row_cut = jnp.broadcast_to(cutoffs, shape[:3]).reshape(-1)
    basis = fourier_basis(jnp.arange(NLON, dtype=jnp.int32), NLON, KMAX)
    coeffs = jnp.dot(flat, basis, precision=lax.Precision.HIGHEST, preferred_element_type=jnp.float32)
    coeffs = coeffs * spectral_weights(row_cut, NLON, KMAX)
    smooth = jnp.dot(coeffs, basis.T, precision=lax.Precision.HIGHEST, preferred_element_type=jnp.float32)
    smooth = smooth.reshape(shape)
    return jnp.concatenate([smooth[:, :, :POLAR], stacked[:, :, POLAR:NLAT - POLAR], smooth[:, :, POLAR:]], axis=2)


def reference(thickness, zonal_wind, merid_wind, tracers, cutoffs):
    every_row = jnp.arange(NLAT, dtype=jnp.int32)
    cos_center = center_cos(every_row, NLAT)[:, None]
    wall_center = (every_row < NLAT - 1).astype(jnp.float32)[:, None]
    face_rows = jnp.arange(NLAT + 1, dtype=jnp.int32) - 1
    cos_face = face_cos(face_rows, NLAT)[:, None]
    wall_face = ((face_rows >= 0) & (face_rows < NLAT - 1)).astype(jnp.float32)[:, None]
    pressure = thickness
    zonal = zonal_wind
    merid = merid_wind
    mass_x = jnp.zeros((LEV, NLAT, NLON + 1), jnp.float32)
    mass_y = jnp.zeros((LEV, NLAT + 1, NLON), jnp.float32)
    wind_x = jnp.zeros((LEV, NLAT, NLON + 1), jnp.float32)
    wind_y = jnp.zeros((LEV, NLAT + 1, NLON), jnp.float32)
    for substep in range(SUBSTEPS):
        padded = wrap_pad(pressure, 1)
        here = padded[:, 1:-1, 1:-1]
        zonal = zonal - PRESSURE_PUSH / cos_center * (padded[:, 1:-1, 2:] - here)
        merid = (merid - PRESSURE_PUSH * (padded[:, 2:, 1:-1] - here)) * wall_center
        stacked = polar_filter(jnp.stack([zonal, merid]), cutoffs)
        zonal = stacked[0]
        merid = stacked[1]
        winds = wrap_pad(stacked, 1)
        east_wind = winds[0, :, 1:-1, :-1]
        north_wind = winds[1, :, :-1, 1:-1]
        flux_x = 0.5 * (padded[:, 1:-1, :-1] + padded[:, 1:-1, 1:]) * east_wind
        flux_y = 0.5 * (padded[:, :-1, 1:-1] + padded[:, 1:, 1:-1]) * north_wind * cos_face * wall_face
        pressure = (pressure - DIVERGE_RATE / cos_center * (flux_x[:, :, 1:] - flux_x[:, :, :-1])
                    - DIVERGE_RATE / cos_center * (flux_y[:, 1:, :] - flux_y[:, :-1, :]))
        mass_x = mass_x + flux_x
        mass_y = mass_y + flux_y
        wind_x = wind_x + east_wind
        wind_y = wind_y + north_wind
    courant_x = COURANT_RATE / cos_center * wind_x
    courant_y = COURANT_RATE * wind_y

    def one_tracer(values):
        extended = wrap_pad(values, 3)
        faces_x = ppm_faces(extended[:, 3:-3, :], courant_x, 2, NLON)
        faces_y = ppm_faces(extended[:, :, 3:-3], courant_y, 1, NLAT)
        carried_x = mass_x * faces_x
        carried_y = mass_y * faces_y
        return (values * thickness - DIVERGE_RATE / cos_center * (carried_x[:, :, 1:] - carried_x[:, :, :-1])
                - DIVERGE_RATE / cos_center * (carried_y[:, 1:, :] - carried_y[:, :-1, :]))

    tracer_mass = lax.map(one_tracer, tracers)
    return pressure, zonal, merid, tracer_mass
```

```python
import math

import numpy as np
import jax
import jax.numpy as jnp
from jax import lax
from jax.experimental import pallas as pl
from jax.experimental.pallas import tpu as pltpu
from jax.sharding import PartitionSpec as P

NLON = 5760
KMAX = 512
SUBSTEPS = 3

LAT_EDGE = 85.0 * math.pi / 180.0
PRESSURE_PUSH = 0.08
DIVERGE_RATE = 0.08
COURANT_RATE = 0.3

HALO = 3
SOUTH_PAD = 4
SIDE = 8
VMEM_LIMIT = 56 * 1024 * 1024


def center_cos(global_rows, total_rows):
    return jnp.cos(((2 * global_rows + 1).astype(jnp.float32) / total_rows - 1.0) * LAT_EDGE)


def face_cos(global_rows, total_rows):
    return jnp.cos(((2 * global_rows + 2).astype(jnp.float32) / total_rows - 1.0) * LAT_EDGE)


def shifted(array, axis, by, wrap):
    count = lax.axis_size(axis)
    pairs = [(i, (i + by) % count) for i in range(count) if wrap or 0 <= i + by < count]
    return lax.ppermute(array, axis, pairs)


def split_bf16(values):
    high = values.astype(jnp.bfloat16)
    low = (values - high.astype(jnp.float32)).astype(jnp.bfloat16)
    return high, low


def basis_tables(width, lanes):
    lane = np.arange(lanes)
    column = np.where(lane < (width + lanes) // 2, lane, lane - lanes)
    phase = (column[:, None] * np.arange(KMAX)[None, :]) % NLON
    angle = phase * (2.0 * math.pi / NLON)
    full = np.concatenate([np.cos(angle), np.sin(angle)], axis=1).astype(np.float32)
    own = np.where((lane < width)[:, None], full, np.float32(0))

    def parts(table):
        high = table.astype(jnp.bfloat16)
        low = (table - high.astype(np.float32)).astype(jnp.bfloat16)
        return jnp.asarray(high), jnp.asarray(low)

    return parts(own), parts(np.ascontiguousarray(full.T))


def dot3(values, high_ref, low_ref):
    high, low = split_bf16(values)
    return (
        jnp.dot(high, high_ref[...], preferred_element_type=jnp.float32)
        + jnp.dot(low, high_ref[...], preferred_element_type=jnp.float32)
        + jnp.dot(high, low_ref[...], preferred_element_type=jnp.float32)
    )


def ahead(values, axis):
    return pltpu.roll(values, values.shape[axis] - 1, axis)


def behind(values, axis):
    return pltpu.roll(values, 1, axis)


def push_winds(p, u, v, rows):
    u = u - rows[:, 0:1] * (ahead(p, 1) - p)
    v = (v - PRESSURE_PUSH * (ahead(p, 0) - p)) * rows[:, 1:2]
    return u, v


def edge_columns(first, last, width):
    end = width % 128
    return first.T[:SIDE], last.T[end - SIDE : end]


def side_lanes(east, west, width):
    end = width % 128
    rows = east.shape[1]
    fill = jnp.zeros((end, rows), jnp.float32)
    gap = jnp.zeros((128 - end - 2 * SIDE, rows), jnp.float32)
    return jnp.concatenate([fill, east, gap, west], axis=0).T


def tracer_edges(width, first_ref, last_ref, head_out, tail_out):
    for t in range(first_ref.shape[0]):
        for l in range(first_ref.shape[1]):
            head, tail = edge_columns(first_ref[t, l], last_ref[t, l], width)
            head_out[t, l] = head
            tail_out[t, l] = tail


def field_edges(width, *refs):
    fields, (south, north), (head_out, tail_out, block) = refs[:6], (refs[6:8], refs[8:10]), refs[10:]
    levels, own_rows = fields[0].shape[:2]
    for f in range(3):
        for l in range(levels):
            sides = []
            for end in range(2):
                block[...] = jnp.zeros_like(block)
                block[SOUTH_PAD - HALO : SOUTH_PAD] = south[end][f, l]
                block[SOUTH_PAD : SOUTH_PAD + own_rows] = fields[2 * f + end][l]
                block[SOUTH_PAD + own_rows : SOUTH_PAD + own_rows + HALO] = north[end][f, l]
                sides.append(block[...])
            head, tail = edge_columns(sides[0], sides[1], width)
            head_out[f, l] = head
            tail_out[f, l] = tail


def first_kernel(
    width, p_ref, u_ref, v_ref, south_ref, north_ref, east_ref, west_ref, rows_ref, fh_ref, fl_ref,
    p_out, u_out, v_out, sums_out, ext
):
    own_rows = p_ref.shape[1]
    whole = width // 128 * 128
    wide = []
    for at, ref in enumerate((p_ref, u_ref, v_ref)):
        ext[at] = jnp.zeros(ext.shape[1:], jnp.float32)
        ext[at, SOUTH_PAD - HALO : SOUTH_PAD, :width] = south_ref[at, 0]
        ext[at, SOUTH_PAD : SOUTH_PAD + own_rows, :width] = ref[0]
        ext[at, SOUTH_PAD + own_rows : SOUTH_PAD + own_rows + HALO, :width] = north_ref[at, 0]
        ext[at, :, whole:] = ext[at, :, whole:] + side_lanes(east_ref[at, 0], west_ref[at, 0], width)
        wide.append(ext[at])
    p_out[0] = wide[0]
    u, v = push_winds(*wide, rows_ref[...])
    u_out[0] = u
    v_out[0] = v
    sums_out[0] = dot3(jnp.concatenate([u, v], axis=0), fh_ref, fl_ref)


def step_kernel(first, last, *refs):
    p_ref, u_ref, v_ref, coeff_ref, rows_ref, ih_ref, il_ref = refs[:7]
    refs = refs[7:]
    if not last:
        fh_ref, fl_ref = refs[:2]
        refs = refs[2:]
    if not first:
        sums_in = refs[:4]
        refs = refs[4:]
    sums_out = refs[:4]
    p_out, u_out, v_out = refs[4:7]
    rows = rows_ref[...]
    count = rows.shape[0]
    smooth = dot3(coeff_ref[0], ih_ref, il_ref)
    polar = rows[:, 3:4] > 0.0
    p = p_ref[0]
    u = jnp.where(polar, smooth[:count], u_ref[0])
    v = jnp.where(polar, smooth[count:], v_ref[0])
    flux_x = 0.5 * (p + ahead(p, 1)) * u
    flux_y = (p + ahead(p, 0)) * v * rows[:, 2:3]
    p = p - rows[:, 0:1] * ((flux_x - behind(flux_x, 1)) + (flux_y - behind(flux_y, 0)))
    for at, term in enumerate((flux_x, flux_y, u, v)):
        sums_out[at][0] = term if first else sums_in[at][0] + term
    if last:
        own = slice(SOUTH_PAD, SOUTH_PAD + p_out.shape[1])
        width = p_out.shape[2]
        p_out[0] = p[own, :width]
        u_out[0] = u[own, :width]
        v_out[0] = v[own, :width]
    else:
        p_out[0] = p
        u, v = push_winds(p, u, v, rows)
        u_out[0] = u
        v_out[0] = v
        refs[7][0] = dot3(p, fh_ref, fl_ref)


def tracer_kernel(
    own_rows, width, q_ref, east_ref, west_ref, south_ref, north_ref, thick_ref, fx_ref, fy_ref, ua_ref, va_ref, rows_ref,
    out_ref, ext, edge, flux, cx, xa, xe, xq, cy, ya, ye, yq, row_k
):
    lanes = ext.shape[1]
    whole = width // 128 * 128
    ext_rows = rows_ref.shape[0]

    @pl.when(pl.program_id(1) == 0)
    def _():
        def coefficients(mass, courant):
            size = jnp.abs(courant)
            slope = mass * size * 0.5
            curve = slope * (1.0 - size * (2.0 / 3.0))
            near = (mass - slope - 3.0 * curve) * (1.0 / 12.0)
            far = (slope - 3.0 * curve) * (1.0 / 12.0)
            return near, far, 6.0 * curve

        own = pl.ds(SOUTH_PAD, own_rows)
        k = rows_ref[own, 0:1]
        c = jnp.clip(rows_ref[own, 4:5] * ua_ref[0, own, :], -1.0, 1.0)
        cx[...] = c
        near, far, cell = coefficients(fx_ref[0, own, :] * k, c)
        xa[...] = near
        xe[...] = far
        xq[...] = cell
        faces = pl.ds(SOUTH_PAD - 1, own_rows + 1)
        at = pl.ds(0, own_rows + 1)
        c = jnp.clip(COURANT_RATE * va_ref[0, faces, :], -1.0, 1.0)
        cy[at, :] = c
        near, far, cell = coefficients(fy_ref[0, faces, :], c)
        ya[at, :] = near
        ye[at, :] = far
        yq[at, :] = cell
        row_k[...] = jnp.broadcast_to(k, row_k.shape)

    ext[8 - HALO : 8, 0:width] = south_ref[0, 0]
    ext[8 + own_rows : 8 + own_rows + HALO, 0:width] = north_ref[0, 0]
    ext[8 : 8 + own_rows, 0:width] = q_ref[0, 0]
    tail = ext[8 : 8 + own_rows, whole:lanes]
    sides = side_lanes(east_ref[0, 0], west_ref[0, 0], width)
    lane = lax.broadcasted_iota(jnp.int32, tail.shape, 1)
    ext[8 : 8 + own_rows, whole:lanes] = jnp.where(lane < width - whole, tail, sides)

    for at in range(0, own_rows, 8):
        here = slice(at, at + 8)
        q = ext[8 + at : 16 + at, :]
        q_next = ahead(q, 1)
        a = 7.0 * (q + q_next) - (behind(q, 1) + pltpu.roll(q, lanes - 2, 1))
        positive = cx[here, :] > 0.0
        e = jnp.where(positive, behind(a, 1), ahead(a, 1))
        cell = jnp.where(positive, q, q_next)
        f = xa[here, :] * a + xe[here, :] * e + xq[here, :] * cell
        f = f - behind(f, 1)
        out_ref[0, 0, here, :] = q[:, :width] * thick_ref[0, here, :] - f[:, :width]

    span = own_rows + 8
    for at in range(0, width, 128):
        here = slice(at, min(at + 128, width))

        edge[0:span, here] = 7.0 * (
            ext[6 : 6 + span, here] + ext[7 : 7 + span, here]
        ) - (ext[5 : 5 + span, here] + ext[8 : 8 + span, here])
        n = own_rows + 1
        positive = cy[0:n, here] > 0.0
        e = jnp.where(positive, edge[0:n, here], edge[2 : 2 + n, here])
        cell = jnp.where(positive, ext[7 : 7 + n, here], ext[8 : 8 + n, here])
        flux[0:n, here] = (
            ya[0:n, here] * edge[1 : 1 + n, here] + ye[0:n, here] * e + yq[0:n, here] * cell
        )
        change = flux[1:n, here] - flux[0 : n - 1, here]
        k = row_k[:, : here.stop - here.start]
        out_ref[0, 0, :, here] = out_ref[0, 0, :, here] - k * change


def circle_sums(partial):
    count = lax.axis_size("lon")
    if count != 4 or partial.shape[0] != 2:
        return lax.psum(partial, "lon")
    even = lax.axis_index("lon") % 2 == 0
    sibling = [(i, i ^ 1) for i in range(count)]
    across = [(i, i ^ 2) for i in range(count)]
    kept = jnp.where(even, partial[0], partial[1])
    sent = jnp.where(even, partial[1], partial[0])
    half = kept + lax.ppermute(sent, "lon", sibling)
    half = half + lax.ppermute(half, "lon", across)
    other = lax.ppermute(half, "lon", sibling)
    return jnp.stack([jnp.where(even, half, other), jnp.where(even, other, half)])


def local(thickness, zonal_wind, merid_wind, tracers, cutoffs):
    levels, own_rows, width = thickness.shape
    tracer_count = tracers.shape[0]
    total_rows = own_rows * lax.axis_size("lat")
    lanes = (width // 128 + 1) * 128
    ext_rows = own_rows + 8
    f32 = jnp.float32

    whole = width // 128 * 128
    q_south = shifted(tracers[:, :, -HALO:], "lat", 1, False)
    q_north = shifted(tracers[:, :, :HALO], "lat", -1, False)
    south = shifted(
        jnp.stack([x[:, -HALO:] for x in (thickness, zonal_wind, merid_wind)]), "lat", 1, False
    )
    north = shifted(
        jnp.stack([x[:, :HALO] for x in (thickness, zonal_wind, merid_wind)]), "lat", -1, False
    )
    q_block = (tracer_count, levels, own_rows, 128)
    q_side = jax.ShapeDtypeStruct((tracer_count, levels, SIDE, own_rows), f32)
    q_head, q_tail = pl.pallas_call(
        lambda *refs: tracer_edges(width, *refs),
        grid=(1,),
        in_specs=[
            pl.BlockSpec(q_block, lambda i: (0, 0, 0, 0)),
            pl.BlockSpec(q_block, lambda i: (0, 0, 0, whole // 128)),
        ],
        out_specs=[pl.BlockSpec(q_side.shape, lambda i: (0, 0, 0, 0))] * 2,
        out_shape=[q_side] * 2,
        name="tracer_edges",
    )(tracers, tracers)
    q_west = shifted(q_tail, "lon", 1, True)
    q_east = shifted(q_head, "lon", -1, True)

    side = jax.ShapeDtypeStruct((3, levels, SIDE, ext_rows), f32)
    own_block, cap_block = (levels, own_rows, 128), (3, levels, HALO, 128)
    ends = [0, whole // 128]
    head, tail = pl.pallas_call(
        lambda *refs: field_edges(width, *refs),
        grid=(1,),
        in_specs=[pl.BlockSpec(own_block, lambda i, e=e: (0, 0, e)) for _ in range(3) for e in ends]
        + [pl.BlockSpec(cap_block, lambda i, e=e: (0, 0, 0, e)) for _ in range(2) for e in ends],
        out_specs=[pl.BlockSpec(side.shape, lambda i: (0, 0, 0, 0))] * 2,
        out_shape=[side] * 2,
        scratch_shapes=[pltpu.VMEM((ext_rows, 128), f32)],
        name="field_edges",
    )(
        thickness, thickness, zonal_wind, zonal_wind, merid_wind, merid_wind,
        south, south, north, north,
    )
    west = shifted(tail, "lon", 1, True)
    east = shifted(head, "lon", -1, True)

    global_rows = (
        lax.axis_index("lat") * own_rows - SOUTH_PAD + jnp.arange(ext_rows, dtype=jnp.int32)
    )
    cos_center = center_cos(global_rows, total_rows)
    wall = ((global_rows >= 0) & (global_rows < total_rows - 1)).astype(f32)
    polar = total_rows // 8
    is_polar = ((global_rows >= 0) & (global_rows < polar)) | (
        (global_rows >= total_rows - polar) & (global_rows < total_rows)
    )
    rate = DIVERGE_RATE / cos_center
    columns = [
        rate, wall, 0.5 * face_cos(global_rows, total_rows) * wall, is_polar.astype(f32),
        COURANT_RATE / cos_center,
    ]
    rows = jnp.pad(jnp.stack(columns, axis=1), ((0, 0), (0, 128 - len(columns))))
    slot = jnp.where(global_rows < polar, global_rows, global_rows - total_rows + 2 * polar)
    matches = slot[:, None] == jnp.arange(2 * polar, dtype=jnp.int32)[None, :]
    row_cut = jnp.sum(jnp.where(matches, cutoffs[None, :], 0), axis=1)
    waves = jnp.arange(KMAX, dtype=jnp.int32)
    scaled = jnp.where(waves == 0, 1.0, 2.0).astype(f32) / NLON
    weight = jnp.where(waves[None, :] < row_cut[:, None], scaled[None, :], 0.0)

    step_angle = 2.0 * math.pi / NLON
    phase = (lax.axis_index("lon") * width * waves) % NLON
    turn_cos = jnp.cos(phase.astype(f32) * step_angle)
    turn_sin = jnp.sin(phase.astype(f32) * step_angle)

    def summed(partial):
        a, b = partial[..., :KMAX], partial[..., KMAX:]
        partial = jnp.concatenate(
            [a * turn_cos - b * turn_sin, a * turn_sin + b * turn_cos], axis=-1
        )
        total = circle_sums(partial)
        a, b = total[..., :KMAX], total[..., KMAX:]
        return a * turn_cos + b * turn_sin, b * turn_cos - a * turn_sin

    wave_angle = waves.astype(f32) * step_angle
    next_sin = jnp.sin(wave_angle)
    next_less = -2.0 * jnp.sin(0.5 * wave_angle) ** 2

    (fh, fl), (ih, il) = basis_tables(width, lanes)
    wide_shape = jax.ShapeDtypeStruct((levels, ext_rows, lanes), f32)
    wide_spec = pl.BlockSpec((1, ext_rows, lanes), lambda l: (l, 0, 0))
    once = pl.Buffered(1)
    rows_spec = pl.BlockSpec(rows.shape, lambda l: (0, 0))
    f_spec = pl.BlockSpec(fh.shape, lambda l: (0, 0), pipeline_mode=once)
    i_spec = pl.BlockSpec(ih.shape, lambda l: (0, 0), pipeline_mode=once)
    params = pltpu.CompilerParams(
        dimension_semantics=("arbitrary",), vmem_limit_bytes=VMEM_LIMIT
    )

    def sums_of(count):
        return (
            jax.ShapeDtypeStruct((levels, count, 2 * KMAX), f32),
            pl.BlockSpec((1, count, 2 * KMAX), lambda l: (l, 0, 0)),
        )

    sums_shape, sums_spec = sums_of(2 * ext_rows)
    p_shape, p_spec = sums_of(ext_rows)
    own_spec = pl.BlockSpec((1, own_rows, width), lambda l: (l, 0, 0))
    own_shape = jax.ShapeDtypeStruct((levels, own_rows, width), f32)
    cap_spec = pl.BlockSpec((3, 1, HALO, width), lambda l: (0, l, 0, 0))
    side_spec = pl.BlockSpec((3, 1, SIDE, ext_rows), lambda l: (0, l, 0, 0))
    p, u, v, partial = pl.pallas_call(
        lambda *refs: first_kernel(width, *refs),
        grid=(levels,),
        in_specs=[own_spec] * 3 + [cap_spec] * 2 + [side_spec] * 2 + [rows_spec, f_spec, f_spec],
        out_specs=[wide_spec] * 3 + [sums_spec],
        out_shape=[wide_shape] * 3 + [sums_shape],
        scratch_shapes=[pltpu.VMEM((3, ext_rows, lanes), f32)],
        compiler_params=params,
        name="first_push",
    )(thickness, zonal_wind, merid_wind, south, north, east, west, rows, fh, fl)

    a, b = summed(partial)
    a = a.reshape(levels, 2, ext_rows, KMAX) * weight
    b = b.reshape(levels, 2, ext_rows, KMAX) * weight
    ua, va, ub, vb = a[:, 0], a[:, 1], b[:, 0], b[:, 1]
    sums = ()
    for substep in range(SUBSTEPS):
        first, last = substep == 0, substep == SUBSTEPS - 1
        coeffs = jnp.concatenate(
            [jnp.concatenate([ua, ub], axis=-1), jnp.concatenate([va, vb], axis=-1)], axis=1
        )
        ins = [p, u, v, coeffs, rows, ih, il]
        in_specs = [wide_spec] * 3 + [sums_spec, rows_spec, i_spec, i_spec]
        if not last:
            ins += [fh, fl]
            in_specs += [f_spec, f_spec]
        ins += list(sums)
        in_specs += [wide_spec] * len(sums)
        out_shape = [wide_shape] * 4 + ([own_shape] * 3 if last else [wide_shape] * 3 + [p_shape])
        out_specs = [wide_spec] * 4 + ([own_spec] * 3 if last else [wide_spec] * 3 + [p_spec])

        def body(*refs, first=first, last=last):
            step_kernel(first, last, *refs)

        outs = pl.pallas_call(
            body,
            grid=(levels,),
            in_specs=in_specs,
            out_specs=out_specs,
            out_shape=out_shape,
            compiler_params=params,
            name="substep",
        )(*ins)
        sums = outs[:4]
        p, u, v = outs[4:7]
        if not last:
            pa, pb = summed(outs[7])
            da = next_less * pa + next_sin * pb
            db = next_less * pb - next_sin * pa
            push_u = rate[:, None] * (PRESSURE_PUSH / DIVERGE_RATE) * weight
            push_v = PRESSURE_PUSH * weight
            ua, ub = ua - push_u * da, ub - push_u * db
            va = (va - push_v * (jnp.roll(pa, -1, axis=1) - pa)) * wall[:, None]
            vb = (vb - push_v * (jnp.roll(pb, -1, axis=1) - pb)) * wall[:, None]

    acc_spec = pl.BlockSpec((1, ext_rows, lanes), lambda l, t: (l, 0, 0))
    tracer_mass = pl.pallas_call(
        lambda *refs: tracer_kernel(own_rows, width, *refs),
        grid=(levels, tracer_count),
        in_specs=[
            pl.BlockSpec((1, 1, own_rows, width), lambda l, t: (t, l, 0, 0)),
            pl.BlockSpec((1, 1, SIDE, own_rows), lambda l, t: (t, l, 0, 0)),
            pl.BlockSpec((1, 1, SIDE, own_rows), lambda l, t: (t, l, 0, 0)),
            pl.BlockSpec((1, 1, HALO, width), lambda l, t: (t, l, 0, 0)),
            pl.BlockSpec((1, 1, HALO, width), lambda l, t: (t, l, 0, 0)),
            pl.BlockSpec((1, own_rows, width), lambda l, t: (l, 0, 0)),
            acc_spec, acc_spec, acc_spec, acc_spec,
            pl.BlockSpec(rows.shape, lambda l, t: (0, 0)),
        ],
        out_specs=pl.BlockSpec((1, 1, own_rows, width), lambda l, t: (t, l, 0, 0)),
        out_shape=jax.ShapeDtypeStruct(tracers.shape, f32),
        scratch_shapes=[pltpu.VMEM((own_rows + 16, lanes), f32)]
        + [pltpu.VMEM((own_rows + 16, lanes), f32)] * 2
        + [pltpu.VMEM((own_rows, lanes), f32)] * 4
        + [pltpu.VMEM((own_rows + 8, lanes), f32)] * 4
        + [pltpu.VMEM((own_rows, 128), f32)],
        compiler_params=pltpu.CompilerParams(
            dimension_semantics=("arbitrary", "arbitrary"), vmem_limit_bytes=VMEM_LIMIT
        ),
        name="tracers",
    )(tracers, q_east, q_west, q_south, q_north, thickness, *sums, rows)

    return (p, u, v, tracer_mass)


def solution(mesh):
    return jax.shard_map(
        local,
        mesh=mesh,
        in_specs=(
            P(None, "lat", "lon"),
            P(None, "lat", "lon"),
            P(None, "lat", "lon"),
            P(None, None, "lat", "lon"),
            P(),
        ),
        out_specs=(
            P(None, "lat", "lon"),
            P(None, "lat", "lon"),
            P(None, "lat", "lon"),
            P(None, None, "lat", "lon"),
        ),
        check_vma=False,
    )
```

```python
import math

import numpy as np
import jax
import jax.numpy as jnp
from jax import lax
from jax.experimental import pallas as pl
from jax.experimental.pallas import tpu as pltpu
from jax.sharding import PartitionSpec as P

NLON = 5760
KMAX = 512
SUBSTEPS = 3

LAT_EDGE = 85.0 * math.pi / 180.0
PRESSURE_PUSH = 0.08
DIVERGE_RATE = 0.08
COURANT_RATE = 0.3

HALO = 3
SOUTH_PAD = 4
SIDE = 8
VMEM_LIMIT = 56 * 1024 * 1024


def center_cos(global_rows, total_rows):
    return jnp.cos(((2 * global_rows + 1).astype(jnp.float32) / total_rows - 1.0) * LAT_EDGE)


def face_cos(global_rows, total_rows):
    return jnp.cos(((2 * global_rows + 2).astype(jnp.float32) / total_rows - 1.0) * LAT_EDGE)


def shifted(array, axis, by, wrap):
    count = lax.axis_size(axis)
    pairs = [(i, (i + by) % count) for i in range(count) if wrap or 0 <= i + by < count]
    return lax.ppermute(array, axis, pairs)


def split_bf16(values):
    high = values.astype(jnp.bfloat16)
    low = (values - high.astype(jnp.float32)).astype(jnp.bfloat16)
    return high, low


def basis_table(width, lanes):
    lane = np.arange(lanes)
    column = np.where(lane < (width + lanes) // 2, lane, lane - lanes)
    phase = (column[:, None] * np.arange(KMAX)[None, :]) % NLON
    angle = phase * (2.0 * math.pi / NLON)
    table = np.concatenate([np.cos(angle), np.sin(angle)], axis=1).astype(np.float32)
    high = table.astype(jnp.bfloat16)
    low = (table - high.astype(np.float32)).astype(jnp.bfloat16)
    return jnp.asarray(high), jnp.asarray(low)


def shift_tables(own_rows):
    faces, cells = own_rows + 8, own_rows + 24
    table = np.zeros((5, faces, cells), np.float32)
    for at in range(own_rows + 1):
        for which, move in enumerate((0, -1, 1)):
            centre = 7 + at + move
            table[which, at, centre - 1 : centre + 3] = (-1, 7, 7, -1)
        table[3, at, 7 + at] = 1
        table[4, at, 8 + at] = 1
    table = table.reshape(5 * faces, cells)
    change = np.zeros((own_rows, faces), np.float32)
    for at in range(own_rows):
        change[at, at : at + 2] = (-1, 1)
    double = lambda x: jnp.asarray(np.concatenate([x, x], axis=1).astype(jnp.bfloat16))
    return double(table), double(change)


def dot3(values, high_ref, low_ref, transposed):
    high, low = split_bf16(values)
    sides = (((1,), (1 if transposed else 0,)), ((), ()))

    def dot(x, ref):
        return lax.dot_general(x, ref[...], sides, preferred_element_type=jnp.float32)

    return dot(high, high_ref) + dot(low, high_ref) + dot(high, low_ref)


def two_parts(values):
    return jnp.concatenate(split_bf16(values), axis=0)


def turned(sums, turn_cos, turn_sin):
    a, b = sums[:, :KMAX], sums[:, KMAX:]
    return jnp.concatenate([a * turn_cos - b * turn_sin, a * turn_sin + b * turn_cos], axis=1)


def forward(values, width, rows_ref, waves_ref, bh_ref, bl_ref, kept_out, sent_out):
    lane = lax.broadcasted_iota(jnp.int32, values.shape, 1)
    sums = dot3(jnp.where(lane < width, values, 0.0), bh_ref, bl_ref, False)
    sums = turned(sums, waves_ref[0:1, :], waves_ref[1:2, :])
    half = sums.shape[0] // 2
    even = rows_ref[0:half, 5:6] > 0.0
    kept_out[...] = jnp.where(even, sums[:half], sums[half:])
    sent_out[...] = jnp.where(even, sums[half:], sums[:half])


def ahead(values, axis):
    return pltpu.roll(values, values.shape[axis] - 1, axis)


def behind(values, axis):
    return pltpu.roll(values, 1, axis)


def push_winds(p, u, v, rows):
    u = u - rows[:, 0:1] * (ahead(p, 1) - p)
    v = (v - PRESSURE_PUSH * (ahead(p, 0) - p)) * rows[:, 1:2]
    return u, v


def edge_columns(first, last, width):
    end = width % 128
    return first.T[:SIDE], last.T[end - SIDE : end]


def side_lanes(east, west, width):
    end = width % 128
    rows = east.shape[1]
    fill = jnp.zeros((end, rows), jnp.float32)
    gap = jnp.zeros((128 - end - 2 * SIDE, rows), jnp.float32)
    return jnp.concatenate([fill, east, gap, west], axis=0).T


def tracer_edges(width, first_ref, last_ref, head_out, tail_out):
    for t in range(first_ref.shape[0]):
        for l in range(first_ref.shape[1]):
            head, tail = edge_columns(first_ref[t, l], last_ref[t, l], width)
            head_out[t, l] = head
            tail_out[t, l] = tail


def field_edges(width, *refs):
    fields, (south, north), (head_out, tail_out, block) = refs[:6], (refs[6:8], refs[8:10]), refs[10:]
    levels, own_rows = fields[0].shape[:2]
    for f in range(3):
        for l in range(levels):
            sides = []
            for end in range(2):
                block[...] = jnp.zeros_like(block)
                block[SOUTH_PAD - HALO : SOUTH_PAD] = south[end][f, l]
                block[SOUTH_PAD : SOUTH_PAD + own_rows] = fields[2 * f + end][l]
                block[SOUTH_PAD + own_rows : SOUTH_PAD + own_rows + HALO] = north[end][f, l]
                sides.append(block[...])
            head, tail = edge_columns(sides[0], sides[1], width)
            head_out[f, l] = head
            tail_out[f, l] = tail


def substeps_kernel(
    p_ref, u_ref, v_ref, south_ref, north_ref, east_ref, west_ref, rows_ref, waves_ref, bh_ref,
    bl_ref, p_out, u_out, v_out, fx_out, fy_out, ua_out, va_out, wide, spectrum, big, small,
    send_sem, recv_sem
):
    levels, own_rows, width = p_ref.shape
    whole = width // 128 * 128
    own = slice(SOUTH_PAD, SOUTH_PAD + own_rows)
    count = rows_ref.shape[0]
    me = lax.axis_index("lon")
    sibling = me + 1 - 2 * lax.rem(me, 2)
    across = lax.rem(me + 2, 4)
    mesh_id = pl.DeviceIdType.MESH

    barrier = pltpu.get_barrier_semaphore()
    for partner in (sibling, across):
        pl.semaphore_signal(barrier, inc=1, device_id={"lon": partner}, device_id_type=mesh_id)

    KEPT, SENT, FROM_CORE, FROM_CHIP, LAST_HALF, HALF, TOTAL = range(7)

    def slot(s, l, role):
        return big.at[l, role] if s == 0 else small.at[s - 1, l, role]

    def copy(s, l, stage):
        source, target, partner = (
            (SENT, FROM_CORE, sibling), (HALF, FROM_CHIP, across), (TOTAL, LAST_HALF, sibling)
        )[stage]
        at = (s * levels + l) * 3 + stage
        return pltpu.make_async_remote_copy(
            src_ref=slot(s, l, source),
            dst_ref=slot(s, l, target),
            send_sem=send_sem.at[at],
            recv_sem=recv_sem.at[at],
            device_id={"lon": partner},
            device_id_type=mesh_id,
        )

    def to_chip(s, l):
        copy(s, l, 0).wait()
        slot(s, l, HALF)[...] = slot(s, l, KEPT)[...] + slot(s, l, FROM_CORE)[...]
        copy(s, l, 1).start()

    def to_core(s, l):
        copy(s, l, 1).wait()
        slot(s, l, TOTAL)[...] = slot(s, l, HALF)[...] + slot(s, l, FROM_CHIP)[...]
        copy(s, l, 2).start()

    def send_forward(s, l, values):
        forward(
            values, width, rows_ref, waves_ref, bh_ref, bl_ref, slot(s, l, KEPT), slot(s, l, SENT)
        )
        copy(s, l, 0).start()

    def push(l):
        u, v = push_winds(wide[0, l], wide[1, l], wide[2, l], rows_ref[...])
        wide[1, l] = u
        wide[2, l] = v
        return u, v

    def summed(s, l):
        copy(s, l, 2).wait()
        half, other = slot(s, l, TOTAL)[...], slot(s, l, LAST_HALF)[...]
        even = rows_ref[0 : half.shape[0], 5:6] > 0.0
        total = jnp.concatenate(
            [jnp.where(even, half, other), jnp.where(even, other, half)], axis=0
        )
        return turned(total, waves_ref[0:1, :], -waves_ref[1:2, :])

    def coefficients(s, l):
        total = summed(s, l)
        rows = rows_ref[...]
        wave = lax.broadcasted_iota(jnp.int32, (count, KMAX), 1).astype(jnp.float32)
        weight = jnp.where(wave < rows[:, 6:7], waves_ref[4:5, :], 0.0)
        weight = jnp.concatenate([weight, weight], axis=1)
        if s == 0:
            spectrum[l] = total * jnp.concatenate([weight, weight], axis=0)
            return
        pa, pb = total[:, :KMAX], total[:, KMAX:]
        less, sine = waves_ref[2:3, :], waves_ref[3:4, :]
        east = jnp.concatenate([less * pa + sine * pb, less * pb - sine * pa], axis=1)
        spectrum[l, :count] = spectrum[l, :count] - rows[:, 0:1] * weight * east
        spectrum[l, count:] = (
            spectrum[l, count:] - PRESSURE_PUSH * weight * (ahead(total, 0) - total)
        ) * rows[:, 1:2]

    def step(s, l):
        coefficients(s, l)
        rows = rows_ref[...]
        smooth = dot3(spectrum[l], bh_ref, bl_ref, True)
        polar = rows[:, 3:4] > 0.0
        p = wide[0, l]
        u = jnp.where(polar, smooth[:count], wide[1, l])
        v = jnp.where(polar, smooth[count:], wide[2, l])
        flux_x = 0.5 * (p + ahead(p, 1)) * u
        flux_y = (p + ahead(p, 0)) * v * rows[:, 2:3]
        p = p - rows[:, 0:1] * ((flux_x - behind(flux_x, 1)) + (flux_y - behind(flux_y, 0)))
        for out, term in ((fx_out, flux_x), (fy_out, flux_y), (ua_out, u), (va_out, v)):
            out[l] = term if s == 0 else out[l] + term
        if s == SUBSTEPS - 1:
            p_out[l] = p[own, :width]
            u_out[l] = u[own, :width]
            v_out[l] = v[own, :width]
        else:
            wide[0, l] = p
            wide[1, l] = u
            wide[2, l] = v

    for l in range(levels):
        for at, ref in enumerate((p_ref, u_ref, v_ref)):
            wide[at, l] = jnp.zeros((count, wide.shape[3]), jnp.float32)
            wide[at, l, SOUTH_PAD - HALO : SOUTH_PAD, :width] = south_ref[at, l]
            wide[at, l, own, :width] = ref[l]
            wide[at, l, SOUTH_PAD + own_rows : SOUTH_PAD + own_rows + HALO, :width] = north_ref[at, l]
            wide[at, l, :, whole:] = wide[at, l, :, whole:] + side_lanes(
                east_ref[at, l], west_ref[at, l], width
            )
    pl.semaphore_wait(barrier, 2)

    for l in range(levels):
        both = jnp.concatenate(push(l), axis=0)
        if l > 0:
            to_chip(0, l - 1)
        send_forward(0, l, both)
    to_chip(0, levels - 1)
    for s in range(SUBSTEPS):
        more = s < SUBSTEPS - 1
        to_core(s, 0)
        for l in range(levels):
            step(s, l)
            if l + 1 < levels:
                to_core(s, l + 1)
            if more:
                if l > 0:
                    to_chip(s + 1, l - 1)
                send_forward(s + 1, l, wide[0, l])
                push(l)
        if more:
            to_chip(s + 1, levels - 1)


def tracer_kernel(
    own_rows, width, q_ref, east_ref, west_ref, south_ref, north_ref, thick_ref, fx_ref, fy_ref, ua_ref, va_ref, rows_ref,
    shift_ref, change_ref, out_ref, ext, cx, xa, xe, xq, cy, ya, ye, yq, row_k
):
    lanes = ext.shape[1]
    whole = width // 128 * 128

    @pl.when(pl.program_id(1) == 0)
    def _():
        ext[...] = jnp.zeros_like(ext)
        for ref in (cy, ya, ye, yq):
            ref[...] = jnp.zeros_like(ref)

        def coefficients(mass, courant):
            size = jnp.abs(courant)
            slope = mass * size * 0.5
            curve = slope * (1.0 - size * (2.0 / 3.0))
            near = (mass - slope - 3.0 * curve) * (1.0 / 12.0)
            far = (slope - 3.0 * curve) * (1.0 / 12.0)
            return near, far, 6.0 * curve

        own = pl.ds(SOUTH_PAD, own_rows)
        k = rows_ref[own, 0:1]
        c = jnp.clip(rows_ref[own, 4:5] * ua_ref[0, own, :], -1.0, 1.0)
        cx[...] = c
        near, far, cell = coefficients(fx_ref[0, own, :] * k, c)
        xa[...] = near
        xe[...] = far
        xq[...] = cell
        faces = pl.ds(SOUTH_PAD - 1, own_rows + 1)
        at = pl.ds(0, own_rows + 1)
        c = jnp.clip(COURANT_RATE * va_ref[0, faces, :], -1.0, 1.0)
        cy[at, :] = c
        near, far, cell = coefficients(fy_ref[0, faces, :], c)
        ya[at, :] = near
        ye[at, :] = far
        yq[at, :] = cell
        row_k[...] = jnp.broadcast_to(k, row_k.shape)

    ext[8 - HALO : 8, 0:width] = south_ref[0, 0]
    ext[8 + own_rows : 8 + own_rows + HALO, 0:width] = north_ref[0, 0]
    ext[8 : 8 + own_rows, 0:width] = q_ref[0, 0]
    tail = ext[8 : 8 + own_rows, whole:lanes]
    sides = side_lanes(east_ref[0, 0], west_ref[0, 0], width)
    lane = lax.broadcasted_iota(jnp.int32, tail.shape, 1)
    ext[8 : 8 + own_rows, whole:lanes] = jnp.where(lane < width - whole, tail, sides)

    for at in range(0, own_rows, 8):
        here = slice(at, at + 8)
        q = ext[8 + at : 16 + at, :]
        q_next = ahead(q, 1)
        a = 7.0 * (q + q_next) - (behind(q, 1) + pltpu.roll(q, lanes - 2, 1))
        positive = cx[here, :] > 0.0
        e = jnp.where(positive, behind(a, 1), ahead(a, 1))
        cell = jnp.where(positive, q, q_next)
        f = xa[here, :] * a + xe[here, :] * e + xq[here, :] * cell
        f = f - behind(f, 1)
        out_ref[0, 0, here, :] = q[:, :width] * thick_ref[0, here, :] - f[:, :width]

    faces = own_rows + 8
    for at in range(0, lanes, 256):
        here = slice(at, at + 256)
        parts = two_parts(ext[:, here])
        moved = jnp.dot(shift_ref[...], parts, preferred_element_type=jnp.float32)
        edge, edge_before, edge_after, cell, cell_after = [
            moved[n * faces : (n + 1) * faces] for n in range(5)
        ]
        positive = cy[:, here] > 0.0
        flux = (
            ya[:, here] * edge
            + ye[:, here] * jnp.where(positive, edge_before, edge_after)
            + yq[:, here] * jnp.where(positive, cell, cell_after)
        )
        change = jnp.dot(change_ref[...], two_parts(flux), preferred_element_type=jnp.float32)
        size = min(256, width - at)
        there = slice(at, at + size)
        out_ref[0, 0, :, there] = out_ref[0, 0, :, there] - (row_k[...] * change)[:, :size]


def local(thickness, zonal_wind, merid_wind, tracers, cutoffs):
    levels, own_rows, width = thickness.shape
    tracer_count = tracers.shape[0]
    total_rows = own_rows * lax.axis_size("lat")
    lanes = (width // 128 + 1) * 128
    ext_rows = own_rows + 8
    f32 = jnp.float32

    whole = width // 128 * 128
    q_south = shifted(tracers[:, :, -HALO:], "lat", 1, False)
    q_north = shifted(tracers[:, :, :HALO], "lat", -1, False)
    south = shifted(
        jnp.stack([x[:, -HALO:] for x in (thickness, zonal_wind, merid_wind)]), "lat", 1, False
    )
    north = shifted(
        jnp.stack([x[:, :HALO] for x in (thickness, zonal_wind, merid_wind)]), "lat", -1, False
    )
    q_block = (tracer_count, levels, own_rows, 128)
    q_side = jax.ShapeDtypeStruct((tracer_count, levels, SIDE, own_rows), f32)
    q_head, q_tail = pl.pallas_call(
        lambda *refs: tracer_edges(width, *refs),
        grid=(1,),
        in_specs=[
            pl.BlockSpec(q_block, lambda i: (0, 0, 0, 0)),
            pl.BlockSpec(q_block, lambda i: (0, 0, 0, whole // 128)),
        ],
        out_specs=[pl.BlockSpec(q_side.shape, lambda i: (0, 0, 0, 0))] * 2,
        out_shape=[q_side] * 2,
        name="tracer_edges",
    )(tracers, tracers)
    q_west = shifted(q_tail, "lon", 1, True)
    q_east = shifted(q_head, "lon", -1, True)

    side = jax.ShapeDtypeStruct((3, levels, SIDE, ext_rows), f32)
    own_block, cap_block = (levels, own_rows, 128), (3, levels, HALO, 128)
    ends = [0, whole // 128]
    head, tail = pl.pallas_call(
        lambda *refs: field_edges(width, *refs),
        grid=(1,),
        in_specs=[pl.BlockSpec(own_block, lambda i, e=e: (0, 0, e)) for _ in range(3) for e in ends]
        + [pl.BlockSpec(cap_block, lambda i, e=e: (0, 0, 0, e)) for _ in range(2) for e in ends],
        out_specs=[pl.BlockSpec(side.shape, lambda i: (0, 0, 0, 0))] * 2,
        out_shape=[side] * 2,
        scratch_shapes=[pltpu.VMEM((ext_rows, 128), f32)],
        name="field_edges",
    )(
        thickness, thickness, zonal_wind, zonal_wind, merid_wind, merid_wind,
        south, south, north, north,
    )
    west = shifted(tail, "lon", 1, True)
    east = shifted(head, "lon", -1, True)

    global_rows = (
        lax.axis_index("lat") * own_rows - SOUTH_PAD + jnp.arange(ext_rows, dtype=jnp.int32)
    )
    cos_center = center_cos(global_rows, total_rows)
    wall = ((global_rows >= 0) & (global_rows < total_rows - 1)).astype(f32)
    polar = total_rows // 8
    is_polar = ((global_rows >= 0) & (global_rows < polar)) | (
        (global_rows >= total_rows - polar) & (global_rows < total_rows)
    )
    rate = DIVERGE_RATE / cos_center
    slot = jnp.where(global_rows < polar, global_rows, global_rows - total_rows + 2 * polar)
    matches = slot[:, None] == jnp.arange(2 * polar, dtype=jnp.int32)[None, :]
    row_cut = jnp.sum(jnp.where(matches, cutoffs[None, :], 0), axis=1)
    even = jnp.broadcast_to(lax.axis_index("lon") % 2 == 0, (ext_rows,))
    columns = [
        rate, wall, 0.5 * face_cos(global_rows, total_rows) * wall, is_polar.astype(f32),
        COURANT_RATE / cos_center, even.astype(f32), row_cut.astype(f32),
    ]
    rows = jnp.pad(jnp.stack(columns, axis=1), ((0, 0), (0, 128 - len(columns))))

    waves = jnp.arange(KMAX, dtype=jnp.int32)
    step_angle = 2.0 * math.pi / NLON
    phase = (lax.axis_index("lon") * width * waves) % NLON
    turn = phase.astype(f32) * step_angle
    wave_angle = waves.astype(f32) * step_angle
    by_wave = [
        jnp.cos(turn), jnp.sin(turn), -2.0 * jnp.sin(0.5 * wave_angle) ** 2, jnp.sin(wave_angle),
        jnp.where(waves == 0, 1.0, 2.0).astype(f32) / NLON,
    ]
    wave_rows = jnp.pad(jnp.stack(by_wave), ((0, 8 - len(by_wave)), (0, 0)))

    bh, bl = basis_table(width, lanes)
    shift, change = shift_tables(own_rows)

    def f32_shape(*shape):
        return jax.ShapeDtypeStruct(shape, f32)

    in_vmem = pl.BlockSpec(memory_space=pltpu.VMEM)
    ins = [
        thickness, zonal_wind, merid_wind, south, north, east, west, rows, wave_rows, bh, bl
    ]
    wide_shape = f32_shape(levels, ext_rows, lanes)
    copies = 3 * SUBSTEPS * levels
    p, u, v, *sums = pl.pallas_call(
        substeps_kernel,
        in_specs=[in_vmem] * len(ins),
        out_specs=[in_vmem] * 7,
        out_shape=[f32_shape(*thickness.shape)] * 3 + [wide_shape] * 4,
        scratch_shapes=[
            pltpu.VMEM((3, levels, ext_rows, lanes), f32),
            pltpu.VMEM((levels, 2 * ext_rows, 2 * KMAX), f32),
            pltpu.VMEM((levels, 7, ext_rows, 2 * KMAX), f32),
            pltpu.VMEM((SUBSTEPS - 1, levels, 7, ext_rows // 2, 2 * KMAX), f32),
            pltpu.SemaphoreType.DMA((copies,)),
            pltpu.SemaphoreType.DMA((copies,)),
        ],
        compiler_params=pltpu.CompilerParams(
            collective_id=0, has_side_effects=True, vmem_limit_bytes=VMEM_LIMIT
        ),
        cost_estimate=pl.CostEstimate(
            flops=30_000_000_000, bytes_accessed=100_000_000, transcendentals=0
        ),
        name="substeps",
    )(*ins)

    def by_tracer(*shape):
        return pl.BlockSpec((1, 1) + shape, lambda l, t: (t, l, 0, 0))

    def by_level(*shape):
        return pl.BlockSpec((1,) + shape, lambda l, t: (l, 0, 0))

    def table(array):
        return pl.BlockSpec(array.shape, lambda l, t: (0, 0))

    tracer_mass = pl.pallas_call(
        lambda *refs: tracer_kernel(own_rows, width, *refs),
        grid=(levels, tracer_count),
        in_specs=[by_tracer(own_rows, width)]
        + [by_tracer(SIDE, own_rows)] * 2
        + [by_tracer(HALO, width)] * 2
        + [by_level(own_rows, width)]
        + [by_level(ext_rows, lanes)] * 4
        + [table(rows), table(shift), table(change)],
        out_specs=by_tracer(own_rows, width),
        out_shape=f32_shape(*tracers.shape),
        scratch_shapes=[pltpu.VMEM((own_rows + 24, lanes), f32)]
        + [pltpu.VMEM((own_rows, lanes), f32)] * 4
        + [pltpu.VMEM((own_rows + 8, lanes), f32)] * 4
        + [pltpu.VMEM((own_rows, 256), f32)],
        compiler_params=pltpu.CompilerParams(
            dimension_semantics=("arbitrary", "arbitrary"), vmem_limit_bytes=VMEM_LIMIT
        ),
        name="tracers",
    )(tracers, q_east, q_west, q_south, q_north, thickness, *sums, rows, shift, change)
    return (p, u, v, tracer_mass)


def solution(mesh):
    return jax.shard_map(
        local,
        mesh=mesh,
        in_specs=(
            P(None, "lat", "lon"),
            P(None, "lat", "lon"),
            P(None, "lat", "lon"),
            P(None, None, "lat", "lon"),
            P(),
        ),
        out_specs=(
            P(None, "lat", "lon"),
            P(None, "lat", "lon"),
            P(None, "lat", "lon"),
            P(None, None, "lat", "lon"),
        ),
        check_vma=False,
    )
```
